32 devices in a mesh: gx: 8 (over z, y), gy: 4 (over x, core).
Axes of the slice: x: 2, y: 2, z: 4, core: 2. Of those that a mesh axis runs over, the one named last changes fastest.
Arguments:
- tokens: bfloat16 [4096, 2048], P('gx', 'gy'), may hold values from -40 to 40
- norm_gain: float32 [2048], replicated, may hold values from 0.25 to 1.75
- expert_ids: int32 [4096, 6], P('gx'), may hold values from 0 to 63, all different within a row; in each aligned block of 512 rows (0 to 511, 512 to 1023, ...) at most 64 rows name the same one
- gate_weights: float32 [4096, 6], P('gx'), may hold values from 0.05 to 0.35
- shared_in: bfloat16 [2, 2048, 2816], P(None, 'gx', 'gy'), may hold values from -0.125 to 0.125
- shared_out: bfloat16 [2816, 2048], P('gy', 'gx'), may hold values from -0.109375 to 0.109375
- expert_in: bfloat16 [64, 2048, 2816], P(('gx', 'gy')), may hold values from -0.125 to 0.125
- expert_out: bfloat16 [64, 1408, 2048], P(('gx', 'gy')), may hold values from -0.15625 to 0.15625
Outputs:
- combined: bfloat16 [4096, 2048], P('gx', 'gy')
The draws below stay inside these ranges and needn't reach their ends.
Inputs may be any that keep to these rules, and one draw needn't show every extreme that they name: `expert_ids`: each row names 6 different experts. In each aligned block of 512 rows (the tokens of one index of gx) no expert is named by more than 64 rows, and in some block one expert is named by exactly 64.
All inputs are finite; a program needn't handle non-finite values.
Results may differ from the reference program's by a relative error of at most 0.017.
Values may be sent and summed in bfloat16 or wider, within the bound.
No kernel may reach another device: no remote copies, remote signals or barrier semaphores. Data moves between devices by JAX's collectives and lax.ppermute only.
A program may use at most 128 MiB of HBM per device.

```python
import math
import jax
import jax.numpy as jnp
import numpy as np
from jax import lax

D = 2048
FF = 1408
EXPERTS = 64
TOPK = 6
SFF = 2816
TOK_DEV = 512
TOKENS = 4096
CAP = 64
FF_SPLIT = 1
FF_PART = 1408
HELD = 2
N_GX = 8
N_GY = 4


def draw_tokens(key, part):
    first, second, third = jax.random.split(key, 3)
    column_scale = jnp.exp(jax.random.uniform(first, (1, D), jnp.float32, 0.0, math.log(10.0)))
    row_scale = jnp.exp(jax.random.uniform(second, (TOKENS, 1), jnp.float32, 0.0, math.log(10.0)))
    base = jax.random.truncated_normal(third, -4.0, 4.0, (TOKENS, D), jnp.float32)
    return (base * row_scale * column_scale * 0.1).astype(jnp.bfloat16)


def block_scale(key, shape, pieces, smallest, top_value):
    gain, own = 1.0, jax.random.fold_in(key, 6)
    for position, blocks in pieces:
        steps = jnp.exp(jax.random.uniform(jax.random.fold_in(own, position), (blocks,), jnp.float32, smallest / len(pieces), top_value / len(pieces)))
        gain = gain * jnp.repeat(steps, shape[position] // blocks).reshape([-1 if axis == position else 1 for axis in range(len(shape))])
    return gain


def routed_block(own_key, own, number, rows, count, top, bound, skew):
    sequence = jax.random.permutation(own_key, count)
    crowded, ordinary = load_shares(count, rows * top, bound, skew, True), load_shares(count, rows * top, bound, skew, False)
    places = jnp.arange(count)

    def named(lengths, offset_by):
        used = int((lengths > 0).sum())
        fixed = max(1, used // 4)
        shifted = fixed + (places - fixed + offset_by * (used - fixed)) % max(1, count - fixed)
        return jnp.zeros((count,), jnp.int32).at[sequence[jnp.where(places < fixed, places, shifted)]].set(jnp.asarray(lengths, jnp.int32))

    lengths = jnp.where(number % 4 == 0, named(crowded, number // 4), named(ordinary, number - number // 4 - 1))
    mixed = jax.random.permutation(jax.random.fold_in(own, 3), count)
    donor, receiver = mixed[0:count // 2 * 2:2], mixed[1:count // 2 * 2:2]
    margin = jnp.minimum(lengths[donor] - 1, bound - lengths[receiver]) // 2
    margin = jnp.where((donor == sequence[0]) | (receiver == sequence[0]) | (lengths[receiver] == 0), 0, jnp.maximum(margin, 0))
    shifted = jax.random.randint(jax.random.fold_in(own, 4), (count // 2,), 0, 1 << 20) % (margin + 1)
    lengths = lengths.at[donor].add(-shifted).at[receiver].add(shifted)
    members = jnp.searchsorted(jnp.cumsum(lengths), jnp.arange(rows * top), side="right").astype(jnp.int32)
    grid = members.reshape(top, rows).T
    grid = grid[jax.random.permutation(jax.random.fold_in(own, 1), rows)]
    offset_by = jax.random.randint(jax.random.fold_in(own, 2), (rows, 1), 0, top)
    return jnp.take_along_axis(grid, (jnp.arange(top)[None, :] + offset_by) % top, axis=1)


def load_shares(amount, total, bound, lean, full):
    portions = [(1 << 20) // math.isqrt(rank ** lean) + 1 for rank in range(1, amount + 1)]
    largest = bound if full else min(bound, max(-(-total // amount), total * portions[0] // sum(portions)))
    least = 1 if total - largest >= amount - 1 else 0
    holding, spare = [largest] + [least] * (amount - 1), total - largest - least * (amount - 1)
    while spare > 0:
        free = [i for i in range(1, amount) if holding[i] < largest] or [i for i in range(1, amount) if holding[i] < bound]
        pool, budget = sum([portions[i] for i in free]), spare
        for i in free:
            addition = min(bound - holding[i], max(1, budget * portions[i] // pool), spare)
            holding[i] = holding[i] + addition
            spare = spare - addition
    return np.array(holding)


def scatter_about(key, extent, spread, reach, cuts=(), kind=jnp.bfloat16):
    level = block_scale(key, extent, cuts, -0.22, 0.18) if cuts else 1.0
    entries = jax.random.normal(key, extent, jnp.float32) * spread * level
    return jnp.minimum(jnp.maximum(entries, -reach), reach).astype(kind)


def setup_inputs(seed: int = 0) -> dict:
    splits = jax.random.split(jax.random.key(seed), 9)
    tokens = draw_tokens(jax.random.fold_in(splits[8], 71), 0)
    norm_gain = jnp.clip(1.0 + 0.15 * jax.random.normal(splits[1], (D,), jnp.float32), 0.25, 1.75)
    expert_ids_keys = jax.random.split(jax.random.fold_in(splits[2], 1), TOKENS // TOK_DEV)
    expert_ids_turns = jax.random.permutation(jax.random.fold_in(splits[2], 3), TOKENS // TOK_DEV)
    expert_ids = jax.vmap(lambda own, number: routed_block(jax.random.fold_in(splits[2], 2), own, number, TOK_DEV, EXPERTS, TOPK, CAP, 2))(expert_ids_keys, expert_ids_turns).reshape((TOKENS, TOPK))
    gate_weights = jnp.clip(0.05 + 0.29999999 * jax.random.uniform(splits[3], (TOKENS, TOPK), jnp.float32) ** block_scale(splits[3], (TOKENS, TOPK), ((0, 8),), -0.2, 0.2), 0.05, 0.35)
    shared_in = scatter_about(splits[4], (2, D, SFF), D ** -0.5, 0.125, ((1, 8), (2, 4)))
    shared_out = scatter_about(splits[5], (SFF, D), SFF ** -0.5, 0.109375, ((0, 4), (1, 8)))
    expert_in = scatter_about(splits[6], (EXPERTS * FF_SPLIT, D, 2 * FF_PART), D ** -0.5, 0.125, ((0, 32),))
    expert_out = scatter_about(splits[7], (EXPERTS * FF_SPLIT, FF_PART, D), FF ** -0.5, 0.15625, ((0, 32),))
    return {"tokens": tokens, "norm_gain": norm_gain, "expert_ids": expert_ids, "gate_weights": gate_weights, "shared_in": shared_in, "shared_out": shared_out, "expert_in": expert_in, "expert_out": expert_out}


epsilon = 1e-06

def reference(tokens, norm_gain, expert_ids, gate_weights, shared_in, shared_out, expert_in, expert_out):
    values = tokens.astype(jnp.float32)
    inverse_rms = lax.rsqrt(lax.optimization_barrier(jnp.mean(values * values, axis=1, keepdims=True)) + epsilon)
    normed = (values * inverse_rms * norm_gain).astype(jnp.bfloat16)
    shared_gate = jnp.dot(normed, shared_in[0], preferred_element_type=jnp.float32)
    shared_up = jnp.dot(normed, shared_in[1], preferred_element_type=jnp.float32)
    shared_hidden = (jax.nn.silu(shared_gate) * shared_up).astype(jnp.bfloat16)
    group_units = SFF // N_GY
    hidden_groups = shared_hidden.reshape(TOKENS, N_GY, group_units).astype(jnp.float32)
    out_groups = shared_out.reshape(N_GY, group_units, D).astype(jnp.float32)
    start_sums = jnp.einsum('tgf,gfd->gtd', hidden_groups, out_groups)
    block_routes = expert_ids.reshape(N_GX, TOK_DEV * TOPK)
    one_hot = (block_routes[:, :, None] == jnp.arange(EXPERTS, dtype=jnp.int32)[None, None, :]).astype(jnp.int32)
    earlier_count = (jnp.cumsum(one_hot, axis=1).astype(jnp.int32) - one_hot).astype(jnp.int32)
    slot_index = lax.optimization_barrier(jnp.sum(earlier_count * one_hot, axis=2)).astype(jnp.int32)
    block_base = (jnp.arange(N_GX, dtype=jnp.int32) * CAP)[:, None]
    slot_place = (block_base + slot_index).astype(jnp.int32).reshape(TOKENS, TOPK)
    token_index = jnp.arange(TOKENS, dtype=jnp.int32)
    buffer_rows = N_GX * CAP
    experts_in = expert_in.reshape(EXPERTS, FF_SPLIT, D, 2 * FF_PART)
    experts_out = expert_out.reshape(EXPERTS, FF_SPLIT, FF_PART, D)
    padded = jnp.concatenate([normed, jnp.zeros((1, D), jnp.bfloat16)], axis=0)

    def one_expert(running, expert):
        chosen = expert_ids == expert
        weight = lax.optimization_barrier(jnp.sum(jnp.where(chosen, gate_weights, jnp.float32(0.0)), axis=1))
        place_here = lax.optimization_barrier(jnp.sum(jnp.where(chosen, slot_place, 0), axis=1)).astype(jnp.int32)
        routed_here = jnp.any(chosen, axis=1)
        target = jnp.where(routed_here, place_here, buffer_rows).astype(jnp.int32)
        source = jnp.full((buffer_rows + 1,), TOKENS, jnp.int32).at[target].set(token_index)[:buffer_rows]
        slot_rows = padded[source]
        weights_in = lax.dynamic_index_in_dim(experts_in, expert, 0, keepdims=False)
        weights_out = lax.dynamic_index_in_dim(experts_out, expert, 0, keepdims=False)
        for slice_number in range(FF_SPLIT):
            gate_up = jnp.dot(slot_rows, weights_in[slice_number], preferred_element_type=jnp.float32)
            hidden = (jax.nn.silu(gate_up[:, :FF_PART]) * gate_up[:, FF_PART:]).astype(jnp.bfloat16)
            piece = jnp.dot(hidden, weights_out[slice_number], preferred_element_type=jnp.float32).astype(jnp.bfloat16)
            piece = lax.optimization_barrier(piece)
            contribution = weight[:, None] * piece.astype(jnp.float32)[place_here]
            group = ((expert * FF_SPLIT + slice_number) // HELD % N_GY).astype(jnp.int32)
            running = running.at[group].add(contribution)
        return (running, None)
    totals, _ = lax.scan(one_expert, start_sums, jnp.arange(EXPERTS, dtype=jnp.int32))
    group_partial = lax.optimization_barrier(totals.astype(jnp.bfloat16))
    return lax.optimization_barrier(jnp.sum(group_partial.astype(jnp.float32), axis=0)).astype(jnp.bfloat16)
```

```python
import jax
import jax.numpy as jnp
from jax import lax
from jax.experimental import pallas as pl
from jax.experimental.pallas import tpu as pltpu
from jax.sharding import PartitionSpec as P

FF = 1408
CAP = 64
META_ROWS = 16
BF16 = jnp.bfloat16
F32 = jnp.float32

epsilon = 1e-06

whole = pl.BlockSpec(memory_space=pltpu.VMEM)


def ring_of(count):
    order = list(range(0, count, 2)) + list(range(1, count, 2))[::-1]
    right = [(order[p], order[(p + 1) % count]) for p in range(count)]
    left = [(b, a) for a, b in right]
    return right, left


def slot_ranks(meta, named, top_count):
    token_count = meta.shape[1]
    hit = jnp.zeros((named.shape[0], token_count), F32)
    for r in range(top_count):
        hit = hit + jnp.where(meta[r : r + 1, :] == named[:, :1], 1.0, 0.0)
    before = lax.broadcasted_iota(jnp.int32, (token_count, token_count), 0) < (
        lax.broadcasted_iota(jnp.int32, (token_count, token_count), 1)
    )
    rank = jnp.dot(hit.astype(BF16), jnp.where(before, 1.0, 0.0).astype(BF16), preferred_element_type=F32)
    return jnp.where(hit > 0.0, rank, -1.0)


def dispatch_kernel(blocks, peers, held, top_count, *refs):
    named_ref = refs[0]
    payloads = refs[1 : 1 + blocks]
    metas = refs[1 + blocks : 1 + 2 * blocks]
    outs = refs[1 + 2 * blocks : 1 + 2 * blocks + peers]
    choose = refs[-1]
    for b in range(blocks):
        meta = metas[b][...].astype(F32)
        token_count = meta.shape[1]
        ranks = slot_ranks(meta, named_ref[...], top_count)
        slot = lax.broadcasted_iota(jnp.int32, (CAP, token_count), 0).astype(F32)
        for c in range(peers * held):
            choose[c * CAP : (c + 1) * CAP, :] = jnp.where(slot == ranks[c : c + 1, :], 1.0, 0.0).astype(BF16)
        rows = jnp.dot(choose[...], payloads[b][:token_count, :], preferred_element_type=F32).astype(BF16)
        for k in range(peers):
            outs[k][b] = rows[k * held * CAP : (k + 1) * held * CAP, :]


def combine_kernel(blocks, incoming, peers, held, top_count, *refs):
    named_ref = refs[0]
    metas = refs[1 : 1 + blocks]
    results = refs[1 + blocks : 1 + blocks + peers]
    coming = refs[1 + blocks + peers : 1 + blocks + peers + incoming]
    outs = refs[1 + blocks + peers + incoming : -2]
    choose, gathered = refs[-2:]
    for b in range(blocks):
        meta = metas[b][...].astype(F32)
        token_count = meta.shape[1]
        named = named_ref[...]
        ranks = slot_ranks(meta, named, top_count)
        weight = jnp.zeros((named.shape[0], token_count), F32)
        for r in range(top_count):
            weight = weight + jnp.where(
                meta[r : r + 1, :] == named[:, :1], meta[top_count + r : top_count + r + 1, :], 0.0
            )
        slot = lax.broadcasted_iota(jnp.int32, (CAP, token_count), 0).astype(F32)
        for c in range(peers * held):
            choose[c * CAP : (c + 1) * CAP, :] = jnp.where(
                slot == ranks[c : c + 1, :], weight[c : c + 1, :], 0.0
            ).astype(BF16)
        for k in range(peers):
            gathered[k * held * CAP : (k + 1) * held * CAP, :] = results[k][b]
        total = lax.dot_general(
            choose[...], gathered[...], (((0,), (0,)), ((), ())), preferred_element_type=F32
        )
        if incoming == blocks:
            total = total + coming[b][...].astype(F32)
        elif blocks == 1:
            for extra in coming:
                total = total + extra[...].astype(F32)
        outs[b][...] = total.astype(BF16)


def expert_kernel(sizes, peers, held, units, features, order_ref, gain_ref, *refs):
    groups = len(sizes)
    parts = refs[: groups * peers]
    in_ref, out_ref = refs[groups * peers : groups * peers + 2]
    outs = refs[groups * peers + 2 : 2 * groups * peers + 2]
    ready, total, hidden = refs[-3:]
    member, step = pl.program_id(0), pl.program_id(1)

    @pl.when(step == 0)
    def _():
        rows = [
            [
                parts[g * peers + k][b, pl.ds(pl.multiple_of(member * CAP, CAP), CAP), :].astype(F32)
                for g in range(groups)
                for b in range(sizes[g])
            ]
            for k in range(peers)
        ]
        for n in range(sum(sizes)):
            squares = jnp.sum(rows[0][n] * rows[0][n], axis=1, keepdims=True)
            for k in range(1, peers):
                squares = squares + jnp.sum(rows[k][n] * rows[k][n], axis=1, keepdims=True)
            inverse_rms = lax.rsqrt(squares / features + epsilon)
            for k in range(peers):
                ready[k, n * CAP : (n + 1) * CAP, :] = (rows[k][n] * inverse_rms * gain_ref[k]).astype(BF16)

    @pl.when(step < peers)
    def _():
        product = jnp.dot(ready[jnp.minimum(step, peers - 1)], in_ref[0], preferred_element_type=F32)

        @pl.when(step == 0)
        def _():
            total[...] = product

        @pl.when(step > 0)
        def _():
            total[...] = total[...] + product

    @pl.when(step == peers - 1)
    def _():
        gate = total[:, :units]
        hidden[...] = (gate / (1.0 + jnp.exp(-gate)) * total[:, units:]).astype(BF16)

    for k in range(peers):

        @pl.when(step == peers + k)
        def _(k=k):
            value = jnp.dot(hidden[...], out_ref[0], preferred_element_type=F32).astype(BF16)
            n = 0
            for g in range(groups):
                for b in range(sizes[g]):
                    outs[g * peers + k][b, pl.ds(pl.multiple_of(member * CAP, CAP), CAP), :] = value[
                        n * CAP : (n + 1) * CAP, :
                    ]
                    n += 1


def shared_kernel(peers, features, order_ref, gain_ref, *refs):
    parts = refs[:peers]
    in_ref, out_ref = refs[peers : peers + 2]
    outs = refs[peers + 2 : 2 * peers + 2]
    ready, gate, up, hidden = refs[-4:]
    step = pl.program_id(0)

    @pl.when(step == 0)
    def _():
        rows = [part[...].astype(F32) for part in parts]
        squares = sum(jnp.sum(r * r, axis=1, keepdims=True) for r in rows)
        inverse_rms = lax.rsqrt(squares / features + epsilon)
        for k in range(peers):
            ready[k] = (rows[k] * inverse_rms * gain_ref[k]).astype(BF16)

    @pl.when(step < peers)
    def _():
        mine = ready[jnp.minimum(step, peers - 1)]
        gate_part = jnp.dot(mine, in_ref[0], preferred_element_type=F32)
        up_part = jnp.dot(mine, in_ref[1], preferred_element_type=F32)

        @pl.when(step == 0)
        def _():
            gate[...] = gate_part
            up[...] = up_part

        @pl.when(step > 0)
        def _():
            gate[...] = gate[...] + gate_part
            up[...] = up[...] + up_part

    @pl.when(step == peers - 1)
    def _():
        value = gate[...]
        hidden[...] = (value / (1.0 + jnp.exp(-value)) * up[...]).astype(BF16)

    for k in range(peers):

        @pl.when(step == peers + k)
        def _(k=k):
            outs[k][...] = jnp.dot(hidden[...], out_ref[...], preferred_element_type=F32).astype(BF16)


def on_device(
    tokens, norm_gain, expert_ids, gate_weights, shared_in, shared_out, expert_in, expert_out
):
    row_count = lax.axis_size("gx")
    peers = lax.axis_size("gy")
    row, column = lax.axis_index("gx"), lax.axis_index("gy")
    token_count, width = tokens.shape
    top_count = expert_ids.shape[1]
    features = norm_gain.shape[0]
    held = expert_in.shape[0]
    units = expert_out.shape[1]
    slice_count = FF // units
    order = jnp.arange(peers, dtype=jnp.int32) ^ column
    gain = norm_gain.reshape(peers, 1, width)[order]
    slices = ((row * peers + order)[:, None] * held + jnp.arange(held, dtype=jnp.int32)).reshape(-1)
    named = jnp.broadcast_to((slices // slice_count).astype(F32)[:, None], (peers * held, 128))

    right, left = ring_of(row_count)

    def to_peer(value, mask):
        return lax.ppermute(value, "gy", [(s, s ^ mask) for s in range(peers)])

    meta = jnp.concatenate(
        [
            expert_ids.T.astype(BF16),
            gate_weights.T.astype(BF16),
            jnp.zeros((META_ROWS - 2 * top_count, token_count), BF16),
        ],
        axis=0,
    )
    payload = jnp.concatenate([tokens, meta.reshape(-1, width)], axis=0)

    from_left, from_right = [payload], [payload]
    for step in range(1, row_count // 2 + 1):
        from_left.append(lax.ppermute(from_left[-1], "gx", right))
        if step < row_count - row_count // 2:
            from_right.append(lax.ppermute(from_right[-1], "gx", left))
    groups = [[payload]]
    for step in range(1, row_count // 2 + 1):
        groups.append([from_left[step]] + ([from_right[step]] if step < len(from_right) else []))
    sizes = [len(group) for group in groups]
    metas = [[p[token_count:].reshape(META_ROWS, token_count) for p in group] for group in groups]

    parts = []
    for group, group_meta in zip(groups, metas):
        blocks = len(group)
        rows = pl.pallas_call(
            lambda *refs, blocks=blocks: dispatch_kernel(blocks, peers, held, top_count, *refs),
            out_shape=[jax.ShapeDtypeStruct((blocks, held * CAP, width), BF16)] * peers,
            in_specs=[whole] * (1 + 2 * blocks),
            out_specs=[whole] * peers,
            scratch_shapes=[pltpu.VMEM((peers * held * CAP, token_count), BF16)],
            compiler_params=pltpu.CompilerParams(vmem_limit_bytes=32 << 20),
            name="dispatch_rows",
        )(named, *group, *group_meta)
        parts += [rows[0]] + [to_peer(rows[k], k) for k in range(1, peers)]

    total_rows = row_count * CAP
    results = pl.pallas_call(
        lambda *refs: expert_kernel(sizes, peers, held, units, features, *refs),
        grid_spec=pltpu.PrefetchScalarGridSpec(
            num_scalar_prefetch=1,
            grid=(held, 2 * peers),
            in_specs=[whole] * (1 + len(parts))
            + [
                pl.BlockSpec((1, width, 2 * units), lambda h, s, o: (h, o[jnp.minimum(s, peers - 1)], 0)),
                pl.BlockSpec((1, units, width), lambda h, s, o: (h, 0, o[jnp.maximum(s - peers, 0)])),
            ],
            out_specs=[whole] * len(parts),
            scratch_shapes=[
                pltpu.VMEM((peers, total_rows, width), BF16),
                pltpu.VMEM((total_rows, 2 * units), F32),
                pltpu.VMEM((total_rows, units), BF16),
            ],
        ),
        out_shape=[jax.ShapeDtypeStruct(part.shape, BF16) for part in parts],
        compiler_params=pltpu.CompilerParams(vmem_limit_bytes=56 << 20),
        name="expert_slices",
    )(order, gain, *parts, expert_in, expert_out)

    pieces = {0: tokens}
    mask = peers // 2
    while mask:
        for k in list(pieces):
            pieces[k ^ mask] = to_peer(pieces[k], mask)
        mask //= 2
    shared_units = shared_out.shape[0]
    shared_parts = pl.pallas_call(
        lambda *refs: shared_kernel(peers, features, *refs),
        grid_spec=pltpu.PrefetchScalarGridSpec(
            num_scalar_prefetch=1,
            grid=(2 * peers,),
            in_specs=[whole] * (1 + peers)
            + [
                pl.BlockSpec((2, width, shared_units), lambda s, o: (0, o[jnp.minimum(s, peers - 1)], 0)),
                pl.BlockSpec((shared_units, width), lambda s, o: (0, o[jnp.maximum(s - peers, 0)])),
            ],
            out_specs=[whole] * peers,
            scratch_shapes=[
                pltpu.VMEM((peers, token_count, width), BF16),
                pltpu.VMEM((token_count, shared_units), F32),
                pltpu.VMEM((token_count, shared_units), F32),
                pltpu.VMEM((token_count, shared_units), BF16),
            ],
        ),
        out_shape=[jax.ShapeDtypeStruct((token_count, width), BF16)] * peers,
        compiler_params=pltpu.CompilerParams(vmem_limit_bytes=40 << 20),
        name="shared_experts",
    )(
        order,
        gain,
        *[pieces[k] for k in range(peers)],
        lax.all_gather(shared_in, "gx", axis=1, tiled=True),
        lax.all_gather(shared_out, "gx", axis=1, tiled=True),
    )
    shared_parts = list(shared_parts)
    mask, last = 1, None
    while mask < peers:
        kept = [k for k in range(0, peers, 2 * mask)]
        arrived = {k: to_peer(shared_parts[k + mask], mask) for k in kept}
        if 2 * mask == peers:
            last = arrived[0]
        else:
            for k in kept:
                shared_parts[k] = (shared_parts[k].astype(F32) + arrived[k].astype(F32)).astype(BF16)
        mask *= 2

    def combine(group_number, coming):
        size = sizes[group_number]
        back = results[group_number * peers : (group_number + 1) * peers]
        back = [back[0]] + [to_peer(back[k], k) for k in range(1, peers)]
        return pl.pallas_call(
            lambda *refs: combine_kernel(size, len(coming), peers, held, top_count, *refs),
            out_shape=[jax.ShapeDtypeStruct((token_count, width), BF16)] * size,
            in_specs=[whole] * (1 + size + peers + len(coming)),
            out_specs=[whole] * size,
            scratch_shapes=[
                pltpu.VMEM((peers * held * CAP, token_count), BF16),
                pltpu.VMEM((peers * held * CAP, width), BF16),
            ],
            compiler_params=pltpu.CompilerParams(vmem_limit_bytes=32 << 20),
            name="combine_rows",
        )(named, *metas[group_number], *back, *coming)

    coming_left, coming_right = None, None
    for step in range(row_count // 2, 0, -1):
        coming = [c for c in (coming_left, coming_right) if c is not None]
        sums = combine(step, coming[:0] if coming_left is None and coming_right is None else
                       ([coming_left if coming_left is not None else jnp.zeros_like(tokens), coming_right]))
        if sizes[step] == 1:
            coming_right, coming_left = lax.ppermute(sums[0], "gx", right), None
        else:
            coming_left = lax.ppermute(sums[0], "gx", left)
            coming_right = lax.ppermute(sums[1], "gx", right)
    return combine(0, [coming_left, coming_right, shared_parts[0], last])[0]


def solution(mesh):
    in_specs = (
        P("gx", "gy"),
        P(),
        P("gx", None),
        P("gx", None),
        P(None, "gx", "gy"),
        P("gy", "gx"),
        P(("gx", "gy"), None, None),
        P(("gx", "gy"), None, None),
    )
    out_specs = P("gx", "gy")
    return jax.shard_map(
        on_device, mesh=mesh, in_specs=in_specs, out_specs=out_specs, check_vma=False
    )
```

```python
import jax
import jax.numpy as jnp
from jax import lax
from jax.experimental import pallas as pl
from jax.experimental.pallas import tpu as pltpu
from jax.sharding import PartitionSpec as P

FF = 1408
CAP = 64
META_ROWS = 16
BF16 = jnp.bfloat16
F32 = jnp.float32

epsilon = 1e-06


def block_of(shape, first=0):
    return pl.BlockSpec(shape, lambda *_: (first,) + (0,) * (len(shape) - 1))


LONG = pl.CostEstimate(flops=40_000_000_000, bytes_accessed=100_000_000, transcendentals=0)


def in_hbm(values):
    return [pltpu.with_memory_space_constraint(v, pltpu.HBM) for v in values]


anywhere = pl.BlockSpec(memory_space=pl.ANY)
smem = pl.BlockSpec(memory_space=pltpu.SMEM)
LANES = 128


def ring_of(count):
    order = list(range(0, count, 2)) + list(range(1, count, 2))[::-1]
    right = [(order[p], order[(p + 1) % count]) for p in range(count)]
    left = [(b, a) for a, b in right]
    return right, left


def slot_ranks(meta, named, top_count):
    token_count = meta.shape[1]
    hit = jnp.zeros((named.shape[0], token_count), F32)
    for r in range(top_count):
        hit = hit + jnp.where(meta[r : r + 1, :] == named[:, :1], 1.0, 0.0)
    before = lax.broadcasted_iota(jnp.int32, (token_count, token_count), 0) < (
        lax.broadcasted_iota(jnp.int32, (token_count, token_count), 1)
    )
    rank = jnp.dot(hit.astype(BF16), jnp.where(before, 1.0, 0.0).astype(BF16), preferred_element_type=F32)
    return jnp.where(hit > 0.0, rank, -1.0)


def dispatch_kernel(forms, peers, held, top_count, *refs):
    named_ref = refs[0]
    blocks = len(forms)
    payloads = refs[1 : 1 + sum(forms)]
    metas = refs[1 + sum(forms) : -2 - peers]
    outs = refs[-2 - peers : -2]
    table, choose = refs[-2:]
    slices = peers * held
    token_count = choose.shape[1]
    first = 0
    for b in range(blocks):
        mine = payloads[first : first + forms[b]]
        first += forms[b]
        meta = (metas[b][...] if metas else mine[0][:META_ROWS]).astype(F32)
        skipped = META_ROWS * token_count // outs[0].shape[2]
        named = named_ref[...]
        ranks = slot_ranks(meta, named, top_count)
        weight = jnp.zeros((named.shape[0], token_count), F32)
        for r in range(top_count):
            weight = weight + jnp.where(
                meta[r : r + 1, :] == named[:, :1], meta[top_count + r : top_count + r + 1, :], 0.0
            )
        table[b, :slices] = ranks
        table[b, slices:] = weight
        slot = lax.broadcasted_iota(jnp.int32, (CAP, token_count), 0).astype(F32)
        for c in range(slices):
            choose[c * CAP : (c + 1) * CAP, :] = jnp.where(slot == ranks[c : c + 1, :], 1.0, 0.0).astype(BF16)
        column, rows = 0, 0.0
        for n, part in enumerate(mine):
            start = 0 if n else skipped
            count = part.shape[0] - start
            rows = rows + jnp.dot(
                choose[:, column : column + count], part[start:, :], preferred_element_type=F32
            )
            column += count
        rows = rows.astype(BF16)
        for k in range(peers):
            outs[k][b] = rows[k * held * CAP : (k + 1) * held * CAP, :]


def combine_kernel(blocks, split, peers, held, *refs):
    table = refs[0]
    results = refs[1 : 1 + peers * held]
    outs = refs[1 + peers * held : -2]
    choose, gathered = refs[-2:]
    slices = peers * held
    for b in range(blocks):
        ranks, weight = table[b, :slices], table[b, slices:]
        token_count = ranks.shape[1]
        half = token_count // 2
        slot = lax.broadcasted_iota(jnp.int32, (CAP, token_count), 0).astype(F32)
        for c in range(slices):
            gathered[c * CAP : (c + 1) * CAP, :] = results[c % held * peers + c // held][b]
            choose[c * CAP : (c + 1) * CAP, :] = jnp.where(
                slot == ranks[c : c + 1, :], weight[c : c + 1, :], 0.0
            ).astype(BF16)
        total = lax.dot_general(
            choose[...], gathered[...], (((0,), (0,)), ((), ())), preferred_element_type=F32
        ).astype(BF16)
        if split:
            outs[0][...] = total[:half]
            outs[1][...] = total[half:]
        else:
            outs[b][...] = total


def expert_kernel(sizes, targets, peers, units, features, order_ref, gain_ref, *refs):
    batches = len(sizes)
    parts = refs[: batches * peers]
    in_ref, out_ref = refs[batches * peers : batches * peers + 2]
    outs = refs[batches * peers + 2 : -3]
    ready, total, hidden = refs[-3:]
    step = pl.program_id(0)

    @pl.when(step == 0)
    def _():
        n = 0
        for g in range(batches):
            for b in range(sizes[g]):
                rows = [parts[g * peers + k][b].astype(F32) for k in range(peers)]
                squares = sum(jnp.sum(r * r, axis=1, keepdims=True) for r in rows)
                inverse_rms = lax.rsqrt(squares / features + epsilon)
                for k in range(peers):
                    ready[k, n * CAP : (n + 1) * CAP, :] = (rows[k] * inverse_rms * gain_ref[k]).astype(BF16)
                n += 1

    @pl.when(step < peers)
    def _():
        product = jnp.dot(ready[jnp.minimum(step, peers - 1)], in_ref[0], preferred_element_type=F32)

        @pl.when(step == 0)
        def _():
            total[...] = product

        @pl.when(step > 0)
        def _():
            total[...] = total[...] + product

    @pl.when(step == peers - 1)
    def _():
        gate = total[:, :units]
        hidden[...] = (gate / (1.0 + jnp.exp(-gate)) * total[:, units:]).astype(BF16)

    for k in range(peers):

        @pl.when(step == peers + k)
        def _(k=k):
            value = jnp.dot(hidden[...], out_ref[0], preferred_element_type=F32).astype(BF16)
            for n, (g, b) in enumerate(targets):
                outs[g * peers + k][b] = value[n * CAP : (n + 1) * CAP, :]


def shared_kernel(peers, features, order_ref, block_ref, gain_ref, *refs):
    parts = refs[:peers]
    *weights, ready, gates, ups, downs, sems = refs[peers:]
    outs = weights[-peers:]
    weights = weights[:-peers]
    blocks = downs.shape[0]
    depth = gates.shape[1] // blocks
    copies = []
    for n in range(blocks):
        start = pl.multiple_of(block_ref[n] * depth, depth)
        columns = (gates.at[:, pl.ds(start, depth)], ups.at[:, pl.ds(start, depth)], downs.at[block_ref[n]])
        for m, target in enumerate(columns):
            source = weights[n].at[m] if n < blocks - 1 or m < 2 else weights[blocks].at[0]
            copies.append(pltpu.make_async_copy(source, target, sems.at[3 * n + m]))
    for copy in copies:
        copy.start()
    rows = [part[...].astype(F32) for part in parts]
    squares = sum(jnp.sum(r * r, axis=1, keepdims=True) for r in rows)
    inverse_rms = lax.rsqrt(squares / features + epsilon)
    for k in range(peers):
        ready[order_ref[k]] = (rows[k] * inverse_rms * gain_ref[k]).astype(BF16)
    for copy in copies:
        copy.wait()
    width = ready.shape[2]
    gate, up = 0.0, 0.0
    across = (((1,), (1,)), ((), ()))
    for q in range(peers):
        columns = slice(q * width, (q + 1) * width)
        gate = gate + lax.dot_general(ready[q], gates[:, columns], across, preferred_element_type=F32)
        up = up + lax.dot_general(ready[q], ups[:, columns], across, preferred_element_type=F32)
    hidden = (gate / (1.0 + jnp.exp(-gate)) * up).astype(BF16)
    each = blocks // peers
    for k in range(peers):
        for m in range(each):
            outs[k][:, m * depth : (m + 1) * depth] = jnp.dot(
                hidden, downs[order_ref[k] * each + m], preferred_element_type=F32
            ).astype(BF16)


def on_device(
    tokens, norm_gain, expert_ids, gate_weights, shared_in, shared_out, expert_in, expert_out
):
    row_count = lax.axis_size("gx")
    peers = lax.axis_size("gy")
    row, column = lax.axis_index("gx"), lax.axis_index("gy")
    token_count, width = tokens.shape
    half = token_count // 2
    far = row_count // 2
    top_count = expert_ids.shape[1]
    features = norm_gain.shape[0]
    held = expert_in.shape[0]
    units = expert_out.shape[1]
    slice_count = FF // units
    slices = peers * held
    order = jnp.arange(peers, dtype=jnp.int32) ^ column
    gain = norm_gain.reshape(peers, 1, width)[order]
    slice_numbers = ((row * peers + order)[:, None] * held + jnp.arange(held, dtype=jnp.int32)).reshape(-1)
    named = jnp.broadcast_to((slice_numbers // slice_count).astype(F32)[:, None], (slices, LANES))

    right, left = ring_of(row_count)

    def to_peer(value, mask):
        return lax.ppermute(value, "gy", [(s, s ^ mask) for s in range(peers)])

    def call(kernel, outs, inputs, scratch, name, in_specs=None, scalars=(), limit=40, cost=None):
        return pl.pallas_call(
            kernel,
            grid=(1,),
            out_shape=[pltpu.HBM(shape, dtype) for shape, dtype in outs],
            in_specs=[smem] * len(scalars) + (in_specs or [block_of(v.shape) for v in inputs]),
            out_specs=[block_of(shape) for shape, _ in outs],
            scratch_shapes=scratch,
            compiler_params=pltpu.CompilerParams(vmem_limit_bytes=limit << 20),
            name=name,
            cost_estimate=cost,
        )(*scalars, *in_hbm(inputs))

    def after(values, *others):
        return lax.optimization_barrier((values, others))[0]

    meta = jnp.concatenate(
        [
            expert_ids.T.astype(BF16),
            gate_weights.T.astype(BF16),
            jnp.zeros((META_ROWS - 2 * top_count, token_count), BF16),
        ],
        axis=0,
    ).reshape(-1, width)
    meta_rows = meta.shape[0]
    payload = jnp.concatenate([meta, tokens], axis=0)

    sizes = [1] + [2] * (far - 1) + [1]
    batches = [[g] for g in range(far + 1)]

    parts, tables = {}, {}

    def dispatch(number, group_blocks):
        blocks = [block for g in batches[number] for block in group_blocks[g]]
        metas = [] if width == token_count else [
            block[0][:meta_rows].reshape(META_ROWS, token_count) for block in blocks
        ]
        *rows, tables[number] = call(
            lambda *refs: dispatch_kernel([len(block) for block in blocks], peers, held, top_count, *refs),
            [((len(blocks), held * CAP, width), BF16)] * peers
            + [((len(blocks), 2 * slices, token_count), F32)],
            [named] + [part for block in blocks for part in block] + metas,
            [pltpu.VMEM((slices * CAP, token_count), BF16)],
            "dispatch_rows",
            cost=LONG,
        )
        parts[number] = [rows[0]] + [to_peer(rows[k], k) for k in range(1, peers)]
        return rows[0]

    groups = {0: [(payload,)]}
    at_left, at_right = payload, payload
    sent = 0
    for step in range(1, far + 1):
        if step < far:
            at_left = lax.ppermute(at_left, "gx", right)
            at_right = lax.ppermute(at_right, "gx", left)
            arrived = [(at_left,), (at_right,)]
        else:
            cut = meta_rows + half
            arrived = [(lax.ppermute(at_left[:cut], "gx", right), lax.ppermute(at_right[cut:], "gx", left))]
        done = [parts[sent - 1]] if sent and step < far else []
        if sent < len(batches) and batches[sent][-1] < step:
            done.append(dispatch(sent, groups))
            sent += 1
        groups[step] = after(arrived, done)
        at_left, at_right = groups[step][0][0], groups[step][-1][-1]
    for number in range(sent, len(batches)):
        last_rows = dispatch(number, groups)

    ring_order = [a for a, _ in right]
    nearby = []
    for i in range(row_count):
        p = ring_order.index(i)
        steps = [0] + [d for s in range(1, far) for d in (-s, s)] + [-far]
        nearby.append([ring_order[(p + d) % row_count] for d in steps])
    block_rows = jnp.asarray(nearby, jnp.int32)[row]
    shared = jnp.concatenate([jnp.swapaxes(shared_in, 1, 2), shared_out[None]], axis=0)
    weights = {0: [shared]}

    def weights_step(step, start):
        left_one, right_one = start
        if step < far:
            weights[step] = [lax.ppermute(left_one, "gx", right), lax.ppermute(right_one, "gx", left)]
        else:
            weights[step] = [
                lax.ppermute(left_one[:2], "gx", right),
                lax.ppermute(right_one[2:], "gx", left),
            ]
        return weights[step]

    listed = list(range(far - 1, 0, -1)) + [far, 0]
    near_groups, far_groups = list(range(far - 2, 0, -1)) + [0], [far - 1, far]

    def places_of(batches_out):
        found = {}
        for number, batch in enumerate(batches_out):
            start = 0
            for g in batch:
                found[g] = (number, start)
                start += sizes[g]
        return found

    def experts(h, inputs, batches_out):
        found = places_of(batches_out)
        counts = [sizes[g] for g in listed]
        targets = [(found[g][0], found[g][1] + b) for g in listed for b in range(sizes[g])]
        outs = [(sum(sizes[g] for g in batch), CAP, width) for batch in batches_out for _ in range(peers)]
        return pl.pallas_call(
            lambda *refs: expert_kernel(counts, targets, peers, units, features, *refs),
            grid_spec=pltpu.PrefetchScalarGridSpec(
                num_scalar_prefetch=1,
                grid=(2 * peers,),
                in_specs=[block_of(gain.shape)]
                + [pl.BlockSpec((part.shape[0], CAP, width), lambda s, o: (0, h, 0)) for part in inputs]
                + [
                    pl.BlockSpec((1, width, 2 * units), lambda s, o: (h, o[jnp.minimum(s, peers - 1)], 0)),
                    pl.BlockSpec((1, units, width), lambda s, o: (h, 0, o[jnp.maximum(s - peers, 0)])),
                ],
                out_specs=[block_of(shape) for shape in outs],
                scratch_shapes=[
                    pltpu.VMEM((peers, row_count * CAP, width), BF16),
                    pltpu.VMEM((row_count * CAP, 2 * units), F32),
                    pltpu.VMEM((row_count * CAP, units), BF16),
                ],
            ),
            out_shape=[pltpu.HBM(shape, BF16) for shape in outs],
            compiler_params=pltpu.CompilerParams(vmem_limit_bytes=56 << 20),
            name="expert_slice",
            cost_estimate=LONG,
        )(order, *in_hbm([gain] + inputs + [expert_in, expert_out]))

    def back(values):
        return [values[0]] + [to_peer(values[k], k) for k in range(1, peers)]

    inputs = [part for g in listed for part in parts[g]]
    ahead = weights_step(1, after((shared, shared), groups[far]))
    inputs, ahead = after((inputs, ahead), last_rows)
    early, next_step = [], 2
    for h in range(held):
        if next_step <= far:
            ahead = weights_step(next_step, ahead)
            next_step += 1
        if h < held - 1:
            result = experts(h, inputs, [listed])
        else:
            result = experts(h, inputs, [far_groups, near_groups])
        result, inputs, early, ahead = after((result, inputs, early, ahead), None)
        if h < held - 1:
            early.append(back(result))
    late = [back(result[:peers]), back(result[peers:])]
    for step in range(next_step, far + 1):
        ahead = weights_step(step, ahead)
    early_places, late_places = places_of([listed]), places_of([far_groups, near_groups])

    pieces = {0: tokens}
    mask = peers // 2
    while mask:
        for k in list(pieces):
            pieces[k ^ mask] = to_peer(pieces[k], mask)
        mask //= 2
    shared_units, depth = shared_out.shape
    shared_parts = call(
        lambda *refs: shared_kernel(peers, features, *refs),
        [((token_count, width), BF16)] * peers,
        [gain] + [pieces[k] for k in range(peers)] + [w for step in range(far + 1) for w in weights[step]],
        [
            pltpu.VMEM((peers, token_count, width), BF16),
            pltpu.VMEM((shared_units, features), BF16),
            pltpu.VMEM((shared_units, features), BF16),
            pltpu.VMEM((row_count, shared_units, depth), BF16),
            pltpu.SemaphoreType.DMA((3 * row_count,)),
        ],
        "shared_experts",
        [block_of(gain.shape)] + [block_of(tokens.shape)] * peers + [anywhere] * (row_count + 1),
        [order, block_rows],
    )
    shared_parts = list(shared_parts)
    mask, last = 1, None
    while mask < peers:
        kept = range(0, peers, 2 * mask)
        arrived = {k: to_peer(shared_parts[k + mask], mask) for k in kept}
        if 2 * mask == peers:
            last = arrived[0]
        else:
            for k in kept:
                shared_parts[k] = (shared_parts[k].astype(F32) + arrived[k].astype(F32)).astype(BF16)
        mask *= 2

    def combine(g):
        size = sizes[g]
        number, place = late_places[g]
        sources = [(member, early_places[g][1]) for member in early] + [(late[number], place)]
        outs = [((half, width), BF16)] * 2 if g == far else [((token_count, width), BF16)] * size
        return call(
            lambda *refs: combine_kernel(size, g == far, peers, held, *refs),
            outs,
            [tables[g]] + [value for values, _ in sources for value in values],
            [pltpu.VMEM((slices * CAP, token_count), BF16), pltpu.VMEM((slices * CAP, width), BF16)],
            "combine_rows",
            [block_of(tables[g].shape)]
            + [block_of((size, CAP, width), start // size) for _, start in sources for _ in range(peers)],
        )

    def add(*values):
        return sum(v.astype(F32) for v in values).astype(BF16)

    top, bottom = combine(far)
    top, bottom = lax.ppermute(top, "gx", right), lax.ppermute(bottom, "gx", left)
    going_left, going_right = combine(far - 1)
    going_left = jnp.concatenate([going_left[:half], add(going_left[half:], bottom)])
    going_right = jnp.concatenate([add(going_right[:half], top), going_right[half:]])
    for g in range(far - 2, -1, -1):
        from_left, from_right = lax.ppermute(going_right, "gx", right), lax.ppermute(going_left, "gx", left)
        own = combine(g)
        if g:
            going_left, going_right = add(own[0], from_right), add(own[1], from_left)
    return add(own[0], from_left, from_right, shared_parts[0], last)


def solution(mesh):
    in_specs = (
        P("gx", "gy"),
        P(),
        P("gx", None),
        P("gx", None),
        P(None, "gx", "gy"),
        P("gy", "gx"),
        P(("gx", "gy"), None, None),
        P(("gx", "gy"), None, None),
    )
    out_specs = P("gx", "gy")
    return jax.shard_map(
        on_device, mesh=mesh, in_specs=in_specs, out_specs=out_specs, check_vma=False
    )
```

```python
import jax
import jax.numpy as jnp
from jax import lax
from jax.experimental import pallas as pl
from jax.experimental.pallas import tpu as pltpu
from jax.sharding import PartitionSpec as P

FF = 1408
CAP = 64
META_ROWS = 16
BF16 = jnp.bfloat16
F32 = jnp.float32

epsilon = 1e-06


def block_of(shape, first=0):
    return pl.BlockSpec(shape, lambda *_: (first,) + (0,) * (len(shape) - 1))


LONG = pl.CostEstimate(flops=40_000_000_000, bytes_accessed=100_000_000, transcendentals=0)


def in_hbm(values):
    return [pltpu.with_memory_space_constraint(v, pltpu.HBM) for v in values]


anywhere = pl.BlockSpec(memory_space=pl.ANY)
smem = pl.BlockSpec(memory_space=pltpu.SMEM)
LANES = 128
ACROSS = (((1,), (1,)), ((), ()))


def ring_of(count):
    order = list(range(0, count, 2)) + list(range(1, count, 2))[::-1]
    right = [(order[p], order[(p + 1) % count]) for p in range(count)]
    left = [(b, a) for a, b in right]
    return right, left


def slot_ranks(meta, named, top_count):
    token_count = meta.shape[1]
    hit = jnp.zeros((named.shape[0], token_count), F32)
    for r in range(top_count):
        hit = hit + jnp.where(meta[r : r + 1, :] == named[:, :1], 1.0, 0.0)
    before = lax.broadcasted_iota(jnp.int32, (token_count, token_count), 0) < (
        lax.broadcasted_iota(jnp.int32, (token_count, token_count), 1)
    )
    rank = jnp.dot(hit.astype(BF16), jnp.where(before, 1.0, 0.0).astype(BF16), preferred_element_type=F32)
    return jnp.where(hit > 0.0, rank, -1.0)


def dispatch_kernel(forms, peers, held, top_count, *refs):
    named_ref = refs[0]
    blocks = len(forms)
    payloads = refs[1 : 1 + sum(forms)]
    metas = refs[1 + sum(forms) : -2 - peers]
    outs = refs[-2 - peers : -2]
    table, choose = refs[-2:]
    slices = peers * held
    token_count = choose.shape[1]
    first = 0
    for b in range(blocks):
        mine = payloads[first : first + forms[b]]
        first += forms[b]
        meta = (metas[b][...] if metas else mine[0][:META_ROWS]).astype(F32)
        skipped = META_ROWS * token_count // outs[0].shape[2]
        named = named_ref[...]
        ranks = slot_ranks(meta, named, top_count)
        weight = jnp.zeros((named.shape[0], token_count), F32)
        for r in range(top_count):
            weight = weight + jnp.where(
                meta[r : r + 1, :] == named[:, :1], meta[top_count + r : top_count + r + 1, :], 0.0
            )
        table[b, :slices] = ranks
        table[b, slices:] = weight
        slot = lax.broadcasted_iota(jnp.int32, (CAP, token_count), 0).astype(F32)
        for c in range(slices):
            choose[c * CAP : (c + 1) * CAP, :] = jnp.where(slot == ranks[c : c + 1, :], 1.0, 0.0).astype(BF16)
        column, rows = 0, 0.0
        for n, part in enumerate(mine):
            start = 0 if n else skipped
            count = part.shape[0] - start
            rows = rows + jnp.dot(
                choose[:, column : column + count], part[start:, :], preferred_element_type=F32
            )
            column += count
        rows = rows.astype(BF16)
        for k in range(peers):
            outs[k][b] = rows[k * held * CAP : (k + 1) * held * CAP, :]


def combine_kernel(blocks, peers, held, *refs):
    table = refs[0]
    results = refs[1 : 1 + peers * held]
    outs = refs[1 + peers * held : -2]
    choose, gathered = refs[-2:]
    slices = peers * held
    for b in range(blocks):
        ranks, weight = table[b, :slices], table[b, slices:]
        token_count = ranks.shape[1]
        half = token_count // 2
        slot = lax.broadcasted_iota(jnp.int32, (CAP, token_count), 0).astype(F32)
        for c in range(slices):
            gathered[c * CAP : (c + 1) * CAP, :] = results[c % held * peers + c // held][b]
            choose[c * CAP : (c + 1) * CAP, :] = jnp.where(
                slot == ranks[c : c + 1, :], weight[c : c + 1, :], 0.0
            ).astype(BF16)
        total = lax.dot_general(
            choose[...], gathered[...], (((0,), (0,)), ((), ())), preferred_element_type=F32
        ).astype(BF16)
        outs[2 * b][...] = total[:half]
        outs[2 * b + 1][...] = total[half:]


def expert_kernel(sizes, targets, peers, units, features, order_ref, gain_ref, *refs):
    batches = len(sizes)
    parts = refs[: batches * peers]
    in_ref, out_ref = refs[batches * peers : batches * peers + 2]
    outs = refs[batches * peers + 2 : -3]
    ready, total, hidden = refs[-3:]
    step = pl.program_id(0)

    @pl.when(step == 0)
    def _():
        n = 0
        for g in range(batches):
            for b in range(sizes[g]):
                rows = [parts[g * peers + k][b].astype(F32) for k in range(peers)]
                squares = sum(jnp.sum(r * r, axis=1, keepdims=True) for r in rows)
                inverse_rms = lax.rsqrt(squares / features + epsilon)
                for k in range(peers):
                    ready[k, n * CAP : (n + 1) * CAP, :] = (rows[k] * inverse_rms * gain_ref[k]).astype(BF16)
                n += 1

    @pl.when(step < peers)
    def _():
        product = jnp.dot(ready[jnp.minimum(step, peers - 1)], in_ref[0], preferred_element_type=F32)

        @pl.when(step == 0)
        def _():
            total[...] = product

        @pl.when(step > 0)
        def _():
            total[...] = total[...] + product

    @pl.when(step == peers - 1)
    def _():
        gate = total[:, :units]
        hidden[...] = (gate / (1.0 + jnp.exp(-gate)) * total[:, units:]).astype(BF16)

    for k in range(peers):

        @pl.when(step == peers + k)
        def _(k=k):
            value = jnp.dot(hidden[...], out_ref[0], preferred_element_type=F32).astype(BF16)
            for n, (g, b) in enumerate(targets):
                outs[g * peers + k][b] = value[n * CAP : (n + 1) * CAP, :]


def shared_first_kernel(peers, features, order_ref, block_ref, gain_ref, *refs):
    parts = refs[:peers]
    *weights, gate, up, last_rows, ready, gates, ups, sems = refs[peers:]
    near = len(weights)
    depth = gates.shape[1] // (near + 1)
    copies = []
    for n in range(near):
        columns = pl.ds(pl.multiple_of(block_ref[n] * depth, depth), depth)
        for m, matrix in enumerate((gates, ups)):
            copies.append(
                pltpu.make_async_copy(weights[n].at[m], matrix.at[:, columns], sems.at[2 * n + m])
            )
    for copy in copies:
        copy.start()
    columns = pl.ds(pl.multiple_of(block_ref[near] * depth, depth), depth)
    for matrix in (gates, ups):
        matrix[:, columns] = jnp.zeros((matrix.shape[0], depth), BF16)
    rows = [part[...].astype(F32) for part in parts]
    squares = sum(jnp.sum(r * r, axis=1, keepdims=True) for r in rows)
    inverse_rms = lax.rsqrt(squares / features + epsilon)
    for k in range(peers):
        ready[order_ref[k]] = (rows[k] * inverse_rms * gain_ref[k]).astype(BF16)
    each = (near + 1) // peers
    start = pl.multiple_of(block_ref[near] % each * depth, depth)
    last_rows[...] = ready[block_ref[near] // each, :, pl.ds(start, depth)]
    for copy in copies:
        copy.wait()
    width = ready.shape[2]
    gate_sum, up_sum = 0.0, 0.0
    for q in range(peers):
        columns = slice(q * width, (q + 1) * width)
        gate_sum = gate_sum + lax.dot_general(ready[q], gates[:, columns], ACROSS, preferred_element_type=F32)
        up_sum = up_sum + lax.dot_general(ready[q], ups[:, columns], ACROSS, preferred_element_type=F32)
    gate[...] = gate_sum
    up[...] = up_sum


def shared_last_kernel(peers, order_ref, block_ref, gate_ref, up_ref, rows_ref, left_ref, right_ref, *refs):
    *weights, downs, sems = refs
    outs = weights[-peers:]
    weights = weights[:-peers]
    near = len(weights)
    depth = downs.shape[2]
    copies = [
        pltpu.make_async_copy(weights[n].at[2], downs.at[block_ref[n]], sems.at[n]) for n in range(near)
    ]
    for copy in copies:
        copy.start()
    gate, up = gate_ref[...], up_ref[...]
    if left_ref.shape[2] < depth:
        cut = left_ref.shape[2]
        for n, half in enumerate((left_ref, right_ref)):
            rows = rows_ref[:, n * cut : (n + 1) * cut]
            gate = gate + lax.dot_general(rows, half[0], ACROSS, preferred_element_type=F32)
            up = up + lax.dot_general(rows, half[1], ACROSS, preferred_element_type=F32)
            downs[block_ref[near], :, n * cut : (n + 1) * cut] = half[2]
    else:
        gate = gate + lax.dot_general(rows_ref[...], left_ref[0], ACROSS, preferred_element_type=F32)
        up = up + lax.dot_general(rows_ref[...], left_ref[1], ACROSS, preferred_element_type=F32)
        downs[block_ref[near]] = right_ref[0]
    hidden = (gate / (1.0 + jnp.exp(-gate)) * up).astype(BF16)
    for copy in copies:
        copy.wait()
    each = (near + 1) // peers
    for k in range(peers):
        for m in range(each):
            outs[k][:, m * depth : (m + 1) * depth] = jnp.dot(
                hidden, downs[order_ref[k] * each + m], preferred_element_type=F32
            ).astype(BF16)


def on_device(
    tokens, norm_gain, expert_ids, gate_weights, shared_in, shared_out, expert_in, expert_out
):
    row_count = lax.axis_size("gx")
    peers = lax.axis_size("gy")
    row, column = lax.axis_index("gx"), lax.axis_index("gy")
    token_count, width = tokens.shape
    half = token_count // 2
    far = row_count // 2
    top_count = expert_ids.shape[1]
    features = norm_gain.shape[0]
    held = expert_in.shape[0]
    units = expert_out.shape[1]
    slice_count = FF // units
    slices = peers * held
    order = jnp.arange(peers, dtype=jnp.int32) ^ column
    gain = norm_gain.reshape(peers, 1, width)[order]
    slice_numbers = ((row * peers + order)[:, None] * held + jnp.arange(held, dtype=jnp.int32)).reshape(-1)
    named = jnp.broadcast_to((slice_numbers // slice_count).astype(F32)[:, None], (slices, LANES))

    right, left = ring_of(row_count)

    def to_peer(value, mask):
        return lax.ppermute(value, "gy", [(s, s ^ mask) for s in range(peers)])

    def call(kernel, outs, inputs, scratch, name, in_specs=None, scalars=(), limit=40, cost=None):
        return pl.pallas_call(
            kernel,
            grid=(1,),
            out_shape=[pltpu.HBM(shape, dtype) for shape, dtype in outs],
            in_specs=[smem] * len(scalars) + (in_specs or [block_of(v.shape) for v in inputs]),
            out_specs=[block_of(shape) for shape, _ in outs],
            scratch_shapes=scratch,
            compiler_params=pltpu.CompilerParams(vmem_limit_bytes=limit << 20),
            name=name,
            cost_estimate=cost,
        )(*scalars, *in_hbm(inputs))

    def after(values, *others):
        return lax.optimization_barrier((values, others))[0]

    meta = jnp.concatenate(
        [
            expert_ids.T.astype(BF16),
            gate_weights.T.astype(BF16),
            jnp.zeros((META_ROWS - 2 * top_count, token_count), BF16),
        ],
        axis=0,
    ).reshape(-1, width)
    meta_rows = meta.shape[0]
    payload = jnp.concatenate([meta, tokens], axis=0)

    sizes = [1] + [2] * (far - 1) + [1]
    batches = [[g] for g in range(far + 1)]

    parts, tables = {}, {}

    def dispatch(number, group_blocks):
        blocks = [block for g in batches[number] for block in group_blocks[g]]
        metas = [] if width == token_count else [
            block[0][:meta_rows].reshape(META_ROWS, token_count) for block in blocks
        ]
        *rows, tables[number] = call(
            lambda *refs: dispatch_kernel([len(block) for block in blocks], peers, held, top_count, *refs),
            [((len(blocks), held * CAP, width), BF16)] * peers
            + [((len(blocks), 2 * slices, token_count), F32)],
            [named] + [part for block in blocks for part in block] + metas,
            [pltpu.VMEM((slices * CAP, token_count), BF16)],
            "dispatch_rows",
            cost=LONG,
        )
        parts[number] = [rows[0]] + [to_peer(rows[k], k) for k in range(1, peers)]
        return rows[0]

    groups = {0: [(payload,)]}
    at_left, at_right = payload, payload
    sent = 0
    for step in range(1, far + 1):
        if step < far:
            at_left = lax.ppermute(at_left, "gx", right)
            at_right = lax.ppermute(at_right, "gx", left)
            arrived = [(at_left,), (at_right,)]
        else:
            cut = meta_rows + half
            arrived = [(lax.ppermute(at_left[:cut], "gx", right), lax.ppermute(at_right[cut:], "gx", left))]
        done = [parts[sent - 1]] if sent and step < far else []
        if sent < len(batches) and batches[sent][-1] < step:
            done.append(dispatch(sent, groups))
            sent += 1
        groups[step] = after(arrived, done)
        at_left, at_right = groups[step][0][0], groups[step][-1][-1]
    for number in range(sent, len(batches)):
        last_rows = dispatch(number, groups)

    ring_order = [a for a, _ in right]
    nearby = []
    for i in range(row_count):
        p = ring_order.index(i)
        steps = [0] + [d for s in range(1, far) for d in (-s, s)] + [-far]
        nearby.append([ring_order[(p + d) % row_count] for d in steps])
    block_rows = jnp.asarray(nearby, jnp.int32)[row]
    shared = jnp.concatenate([jnp.swapaxes(shared_in, 1, 2), shared_out[None]], axis=0)
    weights = {0: [shared]}

    def weights_step(step, start):
        left_one, right_one = start
        if step < far:
            weights[step] = [lax.ppermute(left_one, "gx", right), lax.ppermute(right_one, "gx", left)]
        else:
            cut = shared.shape[2] // 2
            if cut % LANES == 0:
                left_one, right_one = left_one[:, :, :cut], right_one[:, :, cut:]
            else:
                left_one, right_one = left_one[:2], right_one[2:]
            weights[step] = [lax.ppermute(left_one, "gx", right), lax.ppermute(right_one, "gx", left)]
        return weights[step]

    listed = list(range(far - 1, 0, -1)) + [far, 0]
    near_groups, far_groups = list(range(far - 2, 0, -1)) + [0], [far - 1, far]

    def places_of(batches_out):
        found = {}
        for number, batch in enumerate(batches_out):
            start = 0
            for g in batch:
                found[g] = (number, start)
                start += sizes[g]
        return found

    def experts(h, inputs, batches_out):
        found = places_of(batches_out)
        counts = [sizes[g] for g in listed]
        targets = [(found[g][0], found[g][1] + b) for g in listed for b in range(sizes[g])]
        outs = [(sum(sizes[g] for g in batch), CAP, width) for batch in batches_out for _ in range(peers)]
        return pl.pallas_call(
            lambda *refs: expert_kernel(counts, targets, peers, units, features, *refs),
            grid_spec=pltpu.PrefetchScalarGridSpec(
                num_scalar_prefetch=1,
                grid=(2 * peers,),
                in_specs=[block_of(gain.shape)]
                + [pl.BlockSpec((part.shape[0], CAP, width), lambda s, o: (0, h, 0)) for part in inputs]
                + [
                    pl.BlockSpec((1, width, 2 * units), lambda s, o: (h, o[jnp.minimum(s, peers - 1)], 0)),
                    pl.BlockSpec((1, units, width), lambda s, o: (h, 0, o[jnp.maximum(s - peers, 0)])),
                ],
                out_specs=[block_of(shape) for shape in outs],
                scratch_shapes=[
                    pltpu.VMEM((peers, row_count * CAP, width), BF16),
                    pltpu.VMEM((row_count * CAP, 2 * units), F32),
                    pltpu.VMEM((row_count * CAP, units), BF16),
                ],
            ),
            out_shape=[pltpu.HBM(shape, BF16) for shape in outs],
            compiler_params=pltpu.CompilerParams(vmem_limit_bytes=56 << 20),
            name="expert_slice",
            cost_estimate=LONG,
        )(order, *in_hbm([gain] + inputs + [expert_in, expert_out]))

    def back(values):
        return [values[0]] + [to_peer(values[k], k) for k in range(1, peers)]

    inputs = [part for g in listed for part in parts[g]]
    ahead = weights_step(1, after((shared, shared), groups[far - 1]))
    inputs, ahead, own_tokens = after((inputs, ahead, tokens), last_rows)
    pieces = {k: to_peer(own_tokens, k) if k else tokens for k in range(peers)}
    early, next_step = [], 2
    for h in range(held):
        if next_step <= far:
            ahead = weights_step(next_step, ahead)
            next_step += 1
        if h < held - 1:
            result = experts(h, inputs, [listed])
        else:
            result = experts(h, inputs, [far_groups, near_groups])
        result, inputs, early, ahead, pieces = after((result, inputs, early, ahead, pieces), None)
        if h < held - 1:
            early.append(back(result))
    late = [back(result[:peers]), back(result[peers:])]
    for step in range(next_step, far + 1):
        ahead = weights_step(step, ahead)
    early_places, late_places = places_of([listed]), places_of([far_groups, near_groups])

    shared_units, depth = shared_out.shape

    near_weights = [w for step in range(far) for w in weights[step]]
    shared_sums = call(
        lambda *refs: shared_first_kernel(peers, features, *refs),
        [((token_count, shared_units), F32)] * 2 + [((token_count, depth), BF16)],
        [gain] + [pieces[k] for k in range(peers)] + near_weights,
        [
            pltpu.VMEM((peers, token_count, width), BF16),
            pltpu.VMEM((shared_units, features), BF16),
            pltpu.VMEM((shared_units, features), BF16),
            pltpu.SemaphoreType.DMA((2 * (row_count - 1),)),
        ],
        "shared_first",
        in_specs=[block_of(gain.shape)] + [block_of(tokens.shape)] * peers + [anywhere] * (row_count - 1),
        scalars=[order, block_rows],
    )

    def shared_experts():
        inputs = [*shared_sums, *weights[far]]
        return call(
            lambda *refs: shared_last_kernel(peers, *refs),
            [((token_count, width), BF16)] * peers,
            inputs + near_weights,
            [
                pltpu.VMEM((row_count, shared_units, depth), BF16),
                pltpu.SemaphoreType.DMA((row_count - 1,)),
            ],
            "shared_last",
            in_specs=[block_of(v.shape) for v in inputs] + [anywhere] * (row_count - 1),
            scalars=[order, block_rows],
        )

    def reduced(values):
        values = list(values)
        mask = 1
        while True:
            kept = range(0, peers, 2 * mask)
            arrived = {k: to_peer(values[k + mask], mask) for k in kept}
            if 2 * mask == peers:
                return values[0], arrived[0]
            for k in kept:
                values[k] = (values[k].astype(F32) + arrived[k].astype(F32)).astype(BF16)
            mask *= 2

    def combine(g):
        size = sizes[g]
        number, place = late_places[g]
        sources = [(member, early_places[g][1]) for member in early] + [(late[number], place)]
        outs = [((half, width), BF16)] * (2 * size)
        return call(
            lambda *refs: combine_kernel(size, peers, held, *refs),
            outs,
            [tables[g]] + [value for values, _ in sources for value in values],
            [pltpu.VMEM((slices * CAP, token_count), BF16), pltpu.VMEM((slices * CAP, width), BF16)],
            "combine_rows",
            cost=LONG,
            in_specs=[block_of(tables[g].shape)]
            + [block_of((size, CAP, width), start // size) for _, start in sources for _ in range(peers)],
        )

    def add(*values):
        return sum(v.astype(F32) for v in values).astype(BF16)

    def to_right(value):
        return lax.ppermute(value, "gx", right)

    def to_left(value):
        return lax.ppermute(value, "gx", left)

    late[0], weights[far], shared_sums = after((late[0], weights[far], shared_sums), None)
    farthest, sums = combine(far), combine(far - 1)
    first = [to_right(farthest[0]), to_left(farthest[1])]
    left_top, left_bottom, right_top, right_bottom = sums
    left_top, right_bottom = to_left(left_top), to_right(right_bottom)
    shared_parts = shared_experts()
    first, late[1], shared_parts = after((first, late[1], shared_parts), None)
    right_top, left_bottom = to_right(add(right_top, first[0])), to_left(add(left_bottom, first[1]))
    own_part, last_part = reduced(shared_parts)
    for g in range(far - 2, 0, -1):
        sums = combine(g)
        left_top, left_bottom = to_left(add(sums[0], left_top)), to_left(add(sums[1], left_bottom))
        right_top, right_bottom = to_right(add(sums[2], right_top)), to_right(add(sums[3], right_bottom))
    sums = combine(0)
    return jnp.concatenate(
        [
            add(sums[0], left_top, right_top, own_part[:half], last_part[:half]),
            add(sums[1], left_bottom, right_bottom, own_part[half:], last_part[half:]),
        ]
    )


def solution(mesh):
    in_specs = (
        P("gx", "gy"),
        P(),
        P("gx", None),
        P("gx", None),
        P(None, "gx", "gy"),
        P("gy", "gx"),
        P(("gx", "gy"), None, None),
        P(("gx", "gy"), None, None),
    )
    out_specs = P("gx", "gy")
    return jax.shard_map(
        on_device, mesh=mesh, in_specs=in_specs, out_specs=out_specs, check_vma=False
    )
```

```python
import jax
import jax.numpy as jnp
from jax import lax
from jax.experimental import pallas as pl
from jax.experimental.pallas import tpu as pltpu
from jax.sharding import PartitionSpec as P

FF = 1408
CAP = 64
META_ROWS = 16
BF16 = jnp.bfloat16
F32 = jnp.float32

epsilon = 1e-06


def block_of(shape, first=0):
    return pl.BlockSpec(shape, lambda *_: (first,) + (0,) * (len(shape) - 1))


LONG = pl.CostEstimate(flops=40_000_000_000, bytes_accessed=100_000_000, transcendentals=0)


def in_hbm(values):
    return [pltpu.with_memory_space_constraint(v, pltpu.HBM) for v in values]


anywhere = pl.BlockSpec(memory_space=pl.ANY)
smem = pl.BlockSpec(memory_space=pltpu.SMEM)
LANES = 128
ACROSS = (((1,), (1,)), ((), ()))


def ring_of(count):
    order = list(range(0, count, 2)) + list(range(1, count, 2))[::-1]
    right = [(order[p], order[(p + 1) % count]) for p in range(count)]
    left = [(b, a) for a, b in right]
    return right, left


def slot_ranks(meta, named, top_count):
    token_count = meta.shape[1]
    hit = jnp.zeros((named.shape[0], token_count), F32)
    for r in range(top_count):
        hit = hit + jnp.where(meta[r : r + 1, :] == named[:, :1], 1.0, 0.0)
    before = lax.broadcasted_iota(jnp.int32, (token_count, token_count), 0) < (
        lax.broadcasted_iota(jnp.int32, (token_count, token_count), 1)
    )
    rank = jnp.dot(hit.astype(BF16), jnp.where(before, 1.0, 0.0).astype(BF16), preferred_element_type=F32)
    return jnp.where(hit > 0.0, rank, -1.0)


def dispatch_kernel(forms, peers, held, top_count, *refs):
    named_ref = refs[0]
    blocks = len(forms)
    payloads = refs[1 : 1 + sum(forms)]
    metas = refs[1 + sum(forms) : -2 - peers]
    outs = refs[-2 - peers : -2]
    table, choose = refs[-2:]
    slices = peers * held
    token_count = choose.shape[1]
    first = 0
    for b in range(blocks):
        mine = payloads[first : first + forms[b]]
        first += forms[b]
        meta = (metas[b][...] if metas else mine[0][:META_ROWS]).astype(F32)
        skipped = META_ROWS * token_count // outs[0].shape[2]
        named = named_ref[...]
        ranks = slot_ranks(meta, named, top_count)
        weight = jnp.zeros((named.shape[0], token_count), F32)
        for r in range(top_count):
            weight = weight + jnp.where(
                meta[r : r + 1, :] == named[:, :1], meta[top_count + r : top_count + r + 1, :], 0.0
            )
        table[b, :slices] = ranks
        table[b, slices:] = weight
        slot = lax.broadcasted_iota(jnp.int32, (CAP, token_count), 0).astype(F32)
        for c in range(slices):
            choose[c * CAP : (c + 1) * CAP, :] = jnp.where(slot == ranks[c : c + 1, :], 1.0, 0.0).astype(BF16)
        column, rows = 0, 0.0
        for n, part in enumerate(mine):
            start = 0 if n else skipped
            count = part.shape[0] - start
            rows = rows + jnp.dot(
                choose[:, column : column + count], part[start:, :], preferred_element_type=F32
            )
            column += count
        rows = rows.astype(BF16)
        for k in range(peers):
            outs[k][b] = rows[k * held * CAP : (k + 1) * held * CAP, :]


def combine_kernel(blocks, peers, held, *refs):
    table = refs[0]
    results = refs[1 : 1 + peers * held]
    outs = refs[1 + peers * held : -2]
    choose, gathered = refs[-2:]
    slices = peers * held
    for b in range(blocks):
        ranks, weight = table[b, :slices], table[b, slices:]
        token_count = ranks.shape[1]
        half = token_count // 2
        slot = lax.broadcasted_iota(jnp.int32, (CAP, token_count), 0).astype(F32)
        for c in range(slices):
            gathered[c * CAP : (c + 1) * CAP, :] = results[c % held * peers + c // held][b]
            choose[c * CAP : (c + 1) * CAP, :] = jnp.where(
                slot == ranks[c : c + 1, :], weight[c : c + 1, :], 0.0
            ).astype(BF16)
        total = lax.dot_general(
            choose[...], gathered[...], (((0,), (0,)), ((), ())), preferred_element_type=F32
        ).astype(BF16)
        outs[2 * b][...] = total[:half]
        outs[2 * b + 1][...] = total[half:]


def expert_kernel(sizes, targets, peers, units, features, order_ref, gain_ref, *refs):
    batches = len(sizes)
    parts = refs[: batches * peers]
    in_ref, out_ref = refs[batches * peers : batches * peers + 2]
    outs = refs[batches * peers + 2 : -3]
    ready, total, hidden = refs[-3:]
    step = pl.program_id(0)

    @pl.when(step == 0)
    def _():
        n = 0
        for g in range(batches):
            for b in range(sizes[g]):
                rows = [parts[g * peers + k][b].astype(F32) for k in range(peers)]
                squares = sum(jnp.sum(r * r, axis=1, keepdims=True) for r in rows)
                inverse_rms = lax.rsqrt(squares / features + epsilon)
                for k in range(peers):
                    ready[k, n * CAP : (n + 1) * CAP, :] = (rows[k] * inverse_rms * gain_ref[k]).astype(BF16)
                n += 1

    @pl.when(step < peers)
    def _():
        product = jnp.dot(ready[jnp.minimum(step, peers - 1)], in_ref[0], preferred_element_type=F32)

        @pl.when(step == 0)
        def _():
            total[...] = product

        @pl.when(step > 0)
        def _():
            total[...] = total[...] + product

    @pl.when(step == peers - 1)
    def _():
        gate = total[:, :units]
        hidden[...] = (gate / (1.0 + jnp.exp(-gate)) * total[:, units:]).astype(BF16)

    for k in range(peers):

        @pl.when(step == peers + k)
        def _(k=k):
            value = jnp.dot(hidden[...], out_ref[0], preferred_element_type=F32).astype(BF16)
            for n, (g, b) in enumerate(targets):
                outs[g * peers + k][b] = value[n * CAP : (n + 1) * CAP, :]


def shared_first_kernel(peers, features, order_ref, block_ref, gain_ref, *refs):
    parts = refs[:peers]
    *weights, gate, up, last_rows, ready, gates, ups, sems = refs[peers:]
    near = len(weights)
    depth = gates.shape[1] // (near + 1)
    copies = []
    for n in range(near):
        columns = pl.ds(pl.multiple_of(block_ref[n] * depth, depth), depth)
        for m, matrix in enumerate((gates, ups)):
            copies.append(
                pltpu.make_async_copy(weights[n].at[m], matrix.at[:, columns], sems.at[2 * n + m])
            )
    for copy in copies:
        copy.start()
    columns = pl.ds(pl.multiple_of(block_ref[near] * depth, depth), depth)
    for matrix in (gates, ups):
        matrix[:, columns] = jnp.zeros((matrix.shape[0], depth), BF16)
    rows = [part[...].astype(F32) for part in parts]
    squares = sum(jnp.sum(r * r, axis=1, keepdims=True) for r in rows)
    inverse_rms = lax.rsqrt(squares / features + epsilon)
    for k in range(peers):
        ready[order_ref[k]] = (rows[k] * inverse_rms * gain_ref[k]).astype(BF16)
    each = (near + 1) // peers
    start = pl.multiple_of(block_ref[near] % each * depth, depth)
    last_rows[...] = ready[block_ref[near] // each, :, pl.ds(start, depth)]
    for copy in copies:
        copy.wait()
    width = ready.shape[2]
    gate_sum, up_sum = 0.0, 0.0
    for q in range(peers):
        columns = slice(q * width, (q + 1) * width)
        gate_sum = gate_sum + lax.dot_general(ready[q], gates[:, columns], ACROSS, preferred_element_type=F32)
        up_sum = up_sum + lax.dot_general(ready[q], ups[:, columns], ACROSS, preferred_element_type=F32)
    gate[...] = gate_sum
    up[...] = up_sum


def shared_last_kernel(peers, order_ref, block_ref, gate_ref, up_ref, rows_ref, left_ref, right_ref, *refs):
    *weights, downs, sems = refs
    outs = weights[-peers:]
    weights = weights[:-peers]
    near = len(weights)
    depth = downs.shape[2]
    copies = [
        pltpu.make_async_copy(weights[n].at[2], downs.at[block_ref[n]], sems.at[n]) for n in range(near)
    ]
    for copy in copies:
        copy.start()
    gate, up = gate_ref[...], up_ref[...]
    if left_ref.shape[2] < depth:
        cut = left_ref.shape[2]
        for n, half in enumerate((left_ref, right_ref)):
            rows = rows_ref[:, n * cut : (n + 1) * cut]
            gate = gate + lax.dot_general(rows, half[0], ACROSS, preferred_element_type=F32)
            up = up + lax.dot_general(rows, half[1], ACROSS, preferred_element_type=F32)
            downs[block_ref[near], :, n * cut : (n + 1) * cut] = half[2]
    else:
        gate = gate + lax.dot_general(rows_ref[...], left_ref[0], ACROSS, preferred_element_type=F32)
        up = up + lax.dot_general(rows_ref[...], left_ref[1], ACROSS, preferred_element_type=F32)
        downs[block_ref[near]] = right_ref[0]
    hidden = (gate / (1.0 + jnp.exp(-gate)) * up).astype(BF16)
    for copy in copies:
        copy.wait()
    each = (near + 1) // peers
    for k in range(peers):
        for m in range(each):
            outs[k][:, m * depth : (m + 1) * depth] = jnp.dot(
                hidden, downs[order_ref[k] * each + m], preferred_element_type=F32
            ).astype(BF16)


def on_device(
    tokens, norm_gain, expert_ids, gate_weights, shared_in, shared_out, expert_in, expert_out
):
    row_count = lax.axis_size("gx")
    peers = lax.axis_size("gy")
    row, column = lax.axis_index("gx"), lax.axis_index("gy")
    token_count, width = tokens.shape
    half = token_count // 2
    far = row_count // 2
    top_count = expert_ids.shape[1]
    features = norm_gain.shape[0]
    held = expert_in.shape[0]
    units = expert_out.shape[1]
    slice_count = FF // units
    slices = peers * held
    order = jnp.arange(peers, dtype=jnp.int32) ^ column
    gain = norm_gain.reshape(peers, 1, width)[order]
    slice_numbers = ((row * peers + order)[:, None] * held + jnp.arange(held, dtype=jnp.int32)).reshape(-1)
    named = jnp.broadcast_to((slice_numbers // slice_count).astype(F32)[:, None], (slices, LANES))

    right, left = ring_of(row_count)

    def after(values, *others):
        return lax.optimization_barrier((values, others))[0]

    ring_order = [a for a, _ in right]
    nearby = []
    for i in range(row_count):
        p = ring_order.index(i)
        steps = [0] + [d for s in range(1, far) for d in (-s, s)] + [-far]
        nearby.append([ring_order[(p + d) % row_count] for d in steps])
    block_rows = jnp.asarray(nearby, jnp.int32)[row]
    named, order, gain, block_rows = after((named, order, gain, block_rows), None)

    def to_peer(value, mask):
        return lax.ppermute(value, "gy", [(s, s ^ mask) for s in range(peers)])

    def call(kernel, outs, inputs, scratch, name, in_specs=None, scalars=(), limit=40, cost=None):
        return pl.pallas_call(
            kernel,
            grid=(1,),
            out_shape=[pltpu.HBM(shape, dtype) for shape, dtype in outs],
            in_specs=[smem] * len(scalars) + (in_specs or [block_of(v.shape) for v in inputs]),
            out_specs=[block_of(shape) for shape, _ in outs],
            scratch_shapes=scratch,
            compiler_params=pltpu.CompilerParams(vmem_limit_bytes=limit << 20),
            name=name,
            cost_estimate=cost,
        )(*scalars, *in_hbm(inputs))

    meta = jnp.concatenate(
        [
            expert_ids.T.astype(BF16),
            gate_weights.T.astype(BF16),
            jnp.zeros((META_ROWS - 2 * top_count, token_count), BF16),
        ],
        axis=0,
    ).reshape(-1, width)
    meta_rows = meta.shape[0]
    payload = jnp.concatenate([meta, tokens], axis=0)

    sizes = [1] + [2] * (far - 1) + [1]
    batches = [[g] for g in range(far + 1)]

    parts, tables = {}, {}

    def dispatch(number, group_blocks):
        blocks = [block for g in batches[number] for block in group_blocks[g]]
        metas = [] if width == token_count else [
            block[0][:meta_rows].reshape(META_ROWS, token_count) for block in blocks
        ]
        *rows, tables[number] = call(
            lambda *refs: dispatch_kernel([len(block) for block in blocks], peers, held, top_count, *refs),
            [((len(blocks), held * CAP, width), BF16)] * peers
            + [((len(blocks), 2 * slices, token_count), F32)],
            [named] + [part for block in blocks for part in block] + metas,
            [pltpu.VMEM((slices * CAP, token_count), BF16)],
            "dispatch_rows",
            cost=LONG if number < far else None,
        )
        parts[number] = [rows[0]] + [to_peer(rows[k], k) for k in range(1, peers)]
        return rows[0]

    groups = {0: [(payload,)]}
    at_left, at_right = payload, payload
    sent = 0
    for step in range(1, far + 1):
        if step < far:
            at_left = lax.ppermute(at_left, "gx", right)
            at_right = lax.ppermute(at_right, "gx", left)
            arrived = [(at_left,), (at_right,)]
        else:
            cut = meta_rows + half
            arrived = [(lax.ppermute(at_left[:cut], "gx", right), lax.ppermute(at_right[cut:], "gx", left))]
        done = [parts[sent - 1]] if sent and step < far else []
        if sent < len(batches) and batches[sent][-1] < step:
            done.append(dispatch(sent, groups))
            sent += 1
        groups[step] = after(arrived, done)
        at_left, at_right = groups[step][0][0], groups[step][-1][-1]
    for number in range(sent, len(batches)):
        last_rows = dispatch(number, groups)

    shared = jnp.concatenate([jnp.swapaxes(shared_in, 1, 2), shared_out[None]], axis=0)
    weights = {0: [shared]}

    def weights_step(step, start):
        left_one, right_one = start
        if step < far:
            weights[step] = [lax.ppermute(left_one, "gx", right), lax.ppermute(right_one, "gx", left)]
        else:
            cut = shared.shape[2] // 2
            if cut % LANES == 0:
                left_one, right_one = left_one[:, :, :cut], right_one[:, :, cut:]
            else:
                left_one, right_one = left_one[:2], right_one[2:]
            weights[step] = [lax.ppermute(left_one, "gx", right), lax.ppermute(right_one, "gx", left)]
        return weights[step]

    listed = list(range(far - 1, 0, -1)) + [far, 0]
    near_groups, far_groups = list(range(far - 2, 0, -1)) + [0], [far - 1, far]

    def places_of(batches_out):
        found = {}
        for number, batch in enumerate(batches_out):
            start = 0
            for g in batch:
                found[g] = (number, start)
                start += sizes[g]
        return found

    def experts(h, inputs, batches_out):
        found = places_of(batches_out)
        counts = [sizes[g] for g in listed]
        targets = [(found[g][0], found[g][1] + b) for g in listed for b in range(sizes[g])]
        outs = [(sum(sizes[g] for g in batch), CAP, width) for batch in batches_out for _ in range(peers)]
        return pl.pallas_call(
            lambda *refs: expert_kernel(counts, targets, peers, units, features, *refs),
            grid_spec=pltpu.PrefetchScalarGridSpec(
                num_scalar_prefetch=1,
                grid=(2 * peers,),
                in_specs=[block_of(gain.shape)]
                + [pl.BlockSpec((part.shape[0], CAP, width), lambda s, o: (0, h, 0)) for part in inputs]
                + [
                    pl.BlockSpec((1, width, 2 * units), lambda s, o: (h, o[jnp.minimum(s, peers - 1)], 0)),
                    pl.BlockSpec((1, units, width), lambda s, o: (h, 0, o[jnp.maximum(s - peers, 0)])),
                ],
                out_specs=[block_of(shape) for shape in outs],
                scratch_shapes=[
                    pltpu.VMEM((peers, row_count * CAP, width), BF16),
                    pltpu.VMEM((row_count * CAP, 2 * units), F32),
                    pltpu.VMEM((row_count * CAP, units), BF16),
                ],
            ),
            out_shape=[pltpu.HBM(shape, BF16) for shape in outs],
            compiler_params=pltpu.CompilerParams(vmem_limit_bytes=56 << 20),
            name="expert_slice",
            cost_estimate=LONG,
        )(order, *in_hbm([gain] + inputs + [expert_in, expert_out]))

    def back(values):
        return [values[0]] + [to_peer(values[k], k) for k in range(1, peers)]

    inputs = [part for g in listed for part in parts[g]]
    ahead = weights_step(1, after((shared, shared), groups[far - 1]))
    inputs, ahead, own_tokens = after((inputs, ahead, tokens), last_rows)
    pieces = {k: to_peer(own_tokens, k) if k else tokens for k in range(peers)}
    early, next_step = [], 2
    for h in range(held):
        if next_step <= far:
            ahead = weights_step(next_step, ahead)
            next_step += 1
        if h < held - 1:
            result = experts(h, inputs, [listed])
        else:
            result = experts(h, inputs, [far_groups, near_groups])
        result, inputs, early, ahead, pieces = after((result, inputs, early, ahead, pieces), None)
        if h < held - 1:
            early.append(back(result))
    late = [back(result[:peers]), back(result[peers:])]
    for step in range(next_step, far + 1):
        ahead = weights_step(step, ahead)
    early_places, late_places = places_of([listed]), places_of([far_groups, near_groups])

    shared_units, depth = shared_out.shape

    near_weights = [w for step in range(far) for w in weights[step]]
    shared_sums = call(
        lambda *refs: shared_first_kernel(peers, features, *refs),
        [((token_count, shared_units), F32)] * 2 + [((token_count, depth), BF16)],
        [gain] + [pieces[k] for k in range(peers)] + near_weights,
        [
            pltpu.VMEM((peers, token_count, width), BF16),
            pltpu.VMEM((shared_units, features), BF16),
            pltpu.VMEM((shared_units, features), BF16),
            pltpu.SemaphoreType.DMA((2 * (row_count - 1),)),
        ],
        "shared_first",
        in_specs=[block_of(gain.shape)] + [block_of(tokens.shape)] * peers + [anywhere] * (row_count - 1),
        scalars=[order, block_rows],
    )

    def shared_experts():
        inputs = [*shared_sums, *weights[far]]
        return call(
            lambda *refs: shared_last_kernel(peers, *refs),
            [((token_count, width), BF16)] * peers,
            inputs + near_weights,
            [
                pltpu.VMEM((row_count, shared_units, depth), BF16),
                pltpu.SemaphoreType.DMA((row_count - 1,)),
            ],
            "shared_last",
            in_specs=[block_of(v.shape) for v in inputs] + [anywhere] * (row_count - 1),
            scalars=[order, block_rows],
        )

    def reduced(values):
        values = list(values)
        mask = 1
        while True:
            kept = range(0, peers, 2 * mask)
            arrived = {k: to_peer(values[k + mask], mask) for k in kept}
            if 2 * mask == peers:
                return values[0], arrived[0]
            for k in kept:
                values[k] = (values[k].astype(F32) + arrived[k].astype(F32)).astype(BF16)
            mask *= 2

    def combine(g):
        size = sizes[g]
        number, place = late_places[g]
        sources = [(member, early_places[g][1]) for member in early] + [(late[number], place)]
        outs = [((half, width), BF16)] * (2 * size)
        return call(
            lambda *refs: combine_kernel(size, peers, held, *refs),
            outs,
            [tables[g]] + [value for values, _ in sources for value in values],
            [pltpu.VMEM((slices * CAP, token_count), BF16), pltpu.VMEM((slices * CAP, width), BF16)],
            "combine_rows",
            cost=LONG,
            in_specs=[block_of(tables[g].shape)]
            + [block_of((size, CAP, width), start // size) for _, start in sources for _ in range(peers)],
        )

    def add(*values):
        return sum(v.astype(F32) for v in values).astype(BF16)

    def to_right(value):
        return lax.ppermute(value, "gx", right)

    def to_left(value):
        return lax.ppermute(value, "gx", left)

    late[0], weights[far], shared_sums = after((late[0], weights[far], shared_sums), None)
    farthest, sums = combine(far), combine(far - 1)
    first = [to_right(farthest[0]), to_left(farthest[1])]
    left_top, left_bottom, right_top, right_bottom = sums
    left_top, right_bottom = to_left(left_top), to_right(right_bottom)
    shared_parts = shared_experts()
    first, late[1], shared_parts = after((first, late[1], shared_parts), None)
    right_top, left_bottom = to_right(add(right_top, first[0])), to_left(add(left_bottom, first[1]))
    own_part, last_part = reduced(shared_parts)
    for g in range(far - 2, 0, -1):
        sums = combine(g)
        tables[g - 1] = after(tables[g - 1], (left_top, right_top))
        left_top, left_bottom = to_left(add(sums[0], left_top)), to_left(add(sums[1], left_bottom))
        right_top, right_bottom = to_right(add(sums[2], right_top)), to_right(add(sums[3], right_bottom))
    sums = combine(0)
    return jnp.concatenate(
        [
            add(sums[0], left_top, right_top, own_part[:half], last_part[:half]),
            add(sums[1], left_bottom, right_bottom, own_part[half:], last_part[half:]),
        ]
    )


def solution(mesh):
    in_specs = (
        P("gx", "gy"),
        P(),
        P("gx", None),
        P("gx", None),
        P(None, "gx", "gy"),
        P("gy", "gx"),
        P(("gx", "gy"), None, None),
        P(("gx", "gy"), None, None),
    )
    out_specs = P("gx", "gy")
    return jax.shard_map(
        on_device, mesh=mesh, in_specs=in_specs, out_specs=out_specs, check_vma=False
    )
```
